32 devices in a mesh: fsdp: 2 (over x), context: 8 (over z, core), tensor: 2 (over y).
Axes of the slice: x: 2, y: 2, z: 4, core: 2. Of those that a mesh axis runs over, the one named last changes fastest.
Arguments:
- layer_input: bfloat16 [4, 3072, 768], P('fsdp', 'context'), may hold values from -6 to 6
- attention_gain: bfloat16 [768], P('fsdp'), may hold values from 0.099609375 to 1.8984375
- attention_shift: bfloat16 [768], P('fsdp'), may hold values from -1.5 to 1.5
- query_key_value_weight: bfloat16 [768, 3, 768], P('fsdp', None, 'tensor'), may hold values from -0.21875 to 0.21875
- query_key_value_bias: bfloat16 [3, 12, 64], P(None, 'tensor', 'fsdp'), may hold values from -2.5 to 2.5
- attention_output_weight: bfloat16 [768, 768], P('tensor', 'fsdp'), may hold values from -1.25 to 1.25
- output_bias: bfloat16 [768], P('fsdp'), may hold values from -1.5 to 1.5
- feed_gain: bfloat16 [768], P('fsdp'), may hold values from 0.099609375 to 1.8984375
- feed_shift: bfloat16 [768], P('fsdp'), may hold values from -1.5 to 1.5
- up_projection_weight: bfloat16 [768, 3072], P('fsdp', 'tensor'), may hold values from -0.21875 to 0.21875
- up_projection_bias: bfloat16 [48, 64], P('tensor', 'fsdp'), may hold values from -2.5 to 2.5
- down_projection_weight: bfloat16 [3072, 768], P('tensor', 'fsdp'), may hold values from -0.109375 to 0.109375
- down_bias: bfloat16 [768], P('fsdp'), may hold values from -1.5 to 1.5
- cotangent: bfloat16 [4, 3072, 768], P('fsdp', 'context'), may hold values from -6 to 6
Outputs:
- layer_output: bfloat16 [4, 3072, 768], P('fsdp', 'context')
- input_grad: float32 [4, 3072, 768], P('fsdp', 'context')
- grad_attention_gain: float32 [768], P('fsdp')
- grad_attention_shift: float32 [768], P('fsdp')
- grad_heads_weight: float32 [768, 3, 768], P('fsdp', None, 'tensor')
- grad_heads_bias: float32 [3, 12, 64], P(None, 'tensor', 'fsdp')
- grad_output_weight: float32 [768, 768], P('tensor', 'fsdp')
- grad_output_bias: float32 [768], P('fsdp')
- grad_feed_gain: float32 [768], P('fsdp')
- grad_feed_shift: float32 [768], P('fsdp')
- grad_up_weight: float32 [768, 3072], P('fsdp', 'tensor')
- grad_up_bias: float32 [48, 64], P('tensor', 'fsdp')
- grad_down_weight: float32 [3072, 768], P('tensor', 'fsdp')
- grad_down_bias: float32 [768], P('fsdp')
The draws below stay inside these ranges and needn't reach their ends.
All inputs are finite; a program needn't handle non-finite values.
Results may differ from the reference program's by a relative error of at most 0.025.
Values may be sent and summed in bfloat16 or wider, within the bound.
A program may use at most 384 MiB of HBM per device.

```python
import math
import jax
import jax.numpy as jnp
from jax import lax

HEAD_COUNT = 12
HEAD_SIZE = 64
FEED_UNITS = 3072
D = 768
ROT = 16
CTX_TOK = 384
SEQS = 4
SEQ_LEN = 3072
N_CONTEXT = 8


def block_scale(own_key, dims, shards, smallest, high):
    def one(position, shards_of):
        draws = jax.random.uniform(jax.random.fold_in(jax.random.fold_in(own_key, 6), position), (shards_of,), jnp.float32, smallest / len(shards), high / len(shards))
        return jnp.repeat(jnp.exp(draws), dims[position] // shards_of).reshape((-1,) + (1,) * (len(dims) - position - 1))

    factor_of = one(*shards[0])
    for cut in shards[1:]:
        factor_of = factor_of * one(*cut)
    return factor_of


def scatter_about(rng, shape, deviation, limit, split=(), held_as=jnp.bfloat16):
    factor_of = block_scale(rng, shape, split, -0.22, 0.18) if split else 1.0
    drawn = jax.random.normal(rng, shape, jnp.float32) * deviation * factor_of
    return jnp.minimum(jnp.maximum(drawn, -limit), limit).astype(held_as)


def setup_inputs(seed: int = 0) -> dict:
    seeds = jax.random.split(jax.random.key(seed), 15)
    return {
        "layer_input": scatter_about(seeds[0], (SEQS, SEQ_LEN, D), 1.0, 6.0, ((0, 2), (1, 8))),
        "attention_gain": jnp.clip(1.0 + 0.18 * jax.random.normal(seeds[1], (D,), jnp.float32), 0.099609375, 1.8984375).astype(jnp.bfloat16),
        "attention_shift": scatter_about(seeds[2], (D,), 0.3, 1.5, ((0, 2),)),
        "query_key_value_weight": scatter_about(seeds[3], (D, 3, HEAD_COUNT * HEAD_SIZE), D ** -0.5, 0.21875, ((0, 2), (2, 2))),
        "query_key_value_bias": scatter_about(seeds[4], (3, HEAD_COUNT, HEAD_SIZE), 0.5, 2.5, ((1, 2), (2, 2))),
        "attention_output_weight": scatter_about(seeds[5], (HEAD_COUNT * HEAD_SIZE, D), (D // 32) ** -0.5, 1.25, ((0, 2), (1, 2))),
        "output_bias": scatter_about(seeds[6], (D,), 0.3, 1.5, ((0, 2),)),
        "feed_gain": jnp.clip(1.0 + 0.18 * jax.random.normal(seeds[7], (D,), jnp.float32), 0.099609375, 1.8984375).astype(jnp.bfloat16),
        "feed_shift": scatter_about(seeds[8], (D,), 0.3, 1.5, ((0, 2),)),
        "up_projection_weight": scatter_about(seeds[9], (D, FEED_UNITS), D ** -0.5, 0.21875, ((0, 2), (1, 2))),
        "up_projection_bias": scatter_about(seeds[10], (FEED_UNITS // HEAD_SIZE, HEAD_SIZE), 0.5, 2.5, ((0, 2), (1, 2))),
        "down_projection_weight": scatter_about(seeds[11], (FEED_UNITS, D), FEED_UNITS ** -0.5, 0.109375, ((0, 2), (1, 2))),
        "down_bias": scatter_about(seeds[12], (D,), 0.3, 1.5, ((0, 2),)),
        "cotangent": scatter_about(seeds[13], (SEQS, SEQ_LEN, D), 1.0, 6.0, ((0, 2), (1, 8))),
    }


@jax.custom_vjp
def low(v):
    return lax.optimization_barrier(v.astype(jnp.bfloat16)).astype(jnp.float32)

@jax.custom_vjp
def lower_backward(v):
    return v

def low_keep(v):
    return (low(v), None)

def low_pass(kept, grad):
    return (grad,)

def back_keep(v):
    return (v, None)

def back_low(kept, grad):
    return (low(grad),)
low.defvjp(low_keep, low_pass)
lower_backward.defvjp(back_keep, back_low)
norm_eps = 1e-05
rotary_base = 10000.0
masked_score = -1e+30
highest_precision = lax.Precision.HIGHEST

def layer_norm(values, gain, shift):
    center = values - lax.optimization_barrier(jnp.mean(values, axis=-1, keepdims=True))
    spread = lax.optimization_barrier(jnp.mean(center * center, axis=-1, keepdims=True))
    return center * lax.rsqrt(spread + norm_eps) * gain + shift

def rotate(values, cosine, sine_table):
    half_dim = ROT // 2
    leading = values[..., :half_dim]
    trailing = values[..., half_dim:ROT]
    return jnp.concatenate([leading * cosine - trailing * sine_table, trailing * cosine + leading * sine_table, values[..., ROT:]], axis=-1)

def positions():
    row_numbers = jnp.arange(SEQ_LEN, dtype=jnp.int32)
    device_of = row_numbers // CTX_TOK
    within = row_numbers % CTX_TOK
    half_rows = CTX_TOK // 2
    return jnp.where(within < half_rows, device_of * half_rows + within, (2 * N_CONTEXT - 1 - device_of) * half_rows + within - half_rows)

def angles(row_numbers):
    frequency = jnp.power(jnp.float32(rotary_base), -2.0 * jnp.arange(ROT // 2, dtype=jnp.float32) / ROT)
    phases = row_numbers.astype(jnp.float32)[:, None] * frequency[None, :]
    return (jnp.cos(phases)[:, None, :], jnp.sin(phases)[:, None, :])

def attend(queries, key_heads, value_heads, row_numbers):
    block_rows = math.gcd(512, SEQ_LEN)
    inverse_root = 1.0 / math.sqrt(HEAD_SIZE)

    def one_block(block_index):
        offset = block_index * block_rows
        query_rows = lax.dynamic_slice_in_dim(queries, offset, block_rows, 0)
        query_place = lax.dynamic_slice_in_dim(row_numbers, offset, block_rows, 0)
        scores = jnp.einsum('qhd,khd->hqk', query_rows, key_heads, precision=highest_precision)
        scores = lower_backward(scores * inverse_root)
        allowed = row_numbers[None, None, :] <= query_place[None, :, None]
        scores = jnp.where(allowed, scores, masked_score)
        largest = lax.optimization_barrier(jnp.max(scores, axis=-1, keepdims=True))
        weights = jnp.exp(scores - largest)
        weights = weights / lax.optimization_barrier(jnp.sum(weights, axis=-1, keepdims=True))
        return jnp.einsum('hqk,khd->qhd', low(weights), value_heads, precision=highest_precision)
    blocks = lax.map(jax.checkpoint(one_block), jnp.arange(SEQ_LEN // block_rows, dtype=jnp.int32))
    return blocks.reshape(SEQ_LEN, HEAD_COUNT, HEAD_SIZE)

def forward(layer_input, attention_gain, attention_shift, query_key_value_weight, query_key_value_bias, attention_output_weight, output_bias, feed_gain, feed_shift, up_projection_weight, up_projection_bias, down_projection_weight, down_bias):
    row_numbers = positions()
    cosine, sine_table = angles(row_numbers)
    attention_normalized = low(layer_norm(layer_input, attention_gain, attention_shift))
    feed_normalized = low(layer_norm(layer_input, feed_gain, feed_shift))
    projected_heads = jnp.einsum('zkf,fyj->zkyj', attention_normalized, query_key_value_weight, precision=highest_precision) + query_key_value_bias.reshape(3, HEAD_COUNT * HEAD_SIZE)
    projected_heads = lower_backward(projected_heads)
    head_shape = (SEQS, SEQ_LEN, HEAD_COUNT, HEAD_SIZE)
    queries = low(rotate(projected_heads[:, :, 0].reshape(head_shape), cosine, sine_table))
    key_heads = low(rotate(projected_heads[:, :, 1].reshape(head_shape), cosine, sine_table))
    value_heads = low(projected_heads[:, :, 2].reshape(head_shape))
    attention_mixed = lax.map(lambda triple: attend(triple[0], triple[1], triple[2], row_numbers), (queries, key_heads, value_heads))
    attention_mixed = lower_backward(low(attention_mixed.reshape(SEQS, SEQ_LEN, HEAD_COUNT * HEAD_SIZE)))
    hidden_units = lower_backward(jnp.einsum('qmn,ne->qme', feed_normalized, up_projection_weight, precision=highest_precision) + up_projection_bias.reshape(FEED_UNITS))
    gelu_output = low(jax.nn.gelu(hidden_units, approximate=False))
    attention_branch_out = jnp.einsum('zcn,nx->zcx', attention_mixed, attention_output_weight, precision=highest_precision)
    feed_branch_out = jnp.einsum('gbi,iz->gbz', gelu_output, down_projection_weight, precision=highest_precision)
    return layer_input + attention_branch_out + feed_branch_out + output_bias + down_bias

def reference(layer_input, attention_gain, attention_shift, query_key_value_weight, query_key_value_bias, attention_output_weight, output_bias, feed_gain, feed_shift, up_projection_weight, up_projection_bias, down_projection_weight, down_bias, cotangent):
    result, pull_back = jax.vjp(forward, layer_input.astype(jnp.float32), attention_gain.astype(jnp.float32), attention_shift.astype(jnp.float32), query_key_value_weight.astype(jnp.float32), query_key_value_bias.astype(jnp.float32), attention_output_weight.astype(jnp.float32), output_bias.astype(jnp.float32), feed_gain.astype(jnp.float32), feed_shift.astype(jnp.float32), up_projection_weight.astype(jnp.float32), up_projection_bias.astype(jnp.float32), down_projection_weight.astype(jnp.float32), down_bias.astype(jnp.float32))
    grads = pull_back(cotangent.astype(jnp.float32))
    return (result.astype(jnp.bfloat16), grads[0], grads[1], grads[2], grads[3], grads[4], grads[5], grads[6], grads[7], grads[8], grads[9], grads[10], grads[11], grads[12])
```

```python
import math

import jax
import jax.numpy as jnp
from jax import lax
from jax.experimental import pallas as pl
from jax.experimental.pallas import tpu as pltpu
from jax.sharding import PartitionSpec as P

HEAD_SIZE = 64
ROT = 16
PAIR = 2 * HEAD_SIZE


norm_eps = 1e-05
rotary_base = 10000.0
masked_score = -1e30


def dot(a, b, ca, cb):
    return lax.dot_general(a, b, (((ca,), (cb,)), ((), ())), preferred_element_type=jnp.float32)


def attention_kernel(
    members, half, q_ref, do_ref, kv_ref, o_ref, dq_ref, dkv_ref,
    qs, dos, scores, probs, offsets, top, total, acc, dkv
):
    both = 2 * half
    blocks = members // 2
    member = lax.axis_index("context")
    lane = lax.broadcasted_iota(jnp.int32, (half, PAIR), 1)
    first = lane < HEAD_SIZE
    zero = jnp.zeros((half, PAIR), jnp.bfloat16)
    for side in range(2):
        q = q_ref[0, side * half:(side + 1) * half, :]
        g = do_ref[0, side * half:(side + 1) * half, :]
        qs[side, 0:half, :] = jnp.where(first, q, zero)
        qs[side, half:both, :] = jnp.where(first, zero, q)
        dos[side, 0:half, :] = jnp.where(first, g, zero)
        dos[side, half:both, :] = jnp.where(first, zero, g)
    row = lax.broadcasted_iota(jnp.int32, (both, both), 0)
    column = lax.broadcasted_iota(jnp.int32, (both, both), 1)
    offsets[...] = row - jnp.where(column >= half, column - half, column)
    top[...] = jnp.full(top.shape, masked_score, jnp.float32)
    total[...] = jnp.zeros(total.shape, jnp.float32)
    acc[...] = jnp.zeros(acc.shape, jnp.float32)
    dkv[...] = jnp.zeros(dkv.shape, jnp.float32)

    low_jobs = (member + 2) // 2
    jobs = 2 * blocks + 1

    def partial_job(t):
        low = t < low_jobs
        block = jnp.where(low, t, t - low_jobs)
        side = jnp.where(low, 0, 1)
        query_base = jnp.where(low, member, 2 * members - 1 - member) * half
        key_base = jnp.where(low, 0, members * half) + block * both
        first_member = jnp.where(low, 2 * block, members - 1 - 2 * block)
        second_member = jnp.where(low, 2 * block + 1, members - 2 - 2 * block)
        return side, side, first_member, second_member, query_base - key_base

    def load(which, part, a, b):
        return jnp.concatenate([kv_ref[a, which, 0, part], kv_ref[b, which, 0, part]], axis=0)

    def score_job(t, side, part, a, b, limit):
        s = dot(load(0, part, a, b), qs[side], 1, 1)
        if limit is not None:
            s = jnp.where(offsets[...] <= limit, s, masked_score)
        scores[t] = s
        top[side] = jnp.maximum(top[side], jnp.max(s, axis=0, keepdims=True))

    def prob_job(t, side, part, a, b):
        p = jnp.exp(scores[t] - top[side])
        total[side] += jnp.sum(p, axis=0, keepdims=True)
        p = p.astype(jnp.bfloat16)
        probs[t] = p
        acc[side] += dot(load(1, part, a, b), p, 0, 0)

    def back_job(t, side, part, a, b):
        p = probs[t]
        k = load(0, part, a, b)
        dp = dot(load(1, part, a, b), dos[side], 1, 1)
        ds = (p.astype(jnp.float32) * (dp - total[side])).astype(jnp.bfloat16)
        acc[side] += dot(k, ds, 0, 0)
        dk = dot(ds, qs[side], 1, 0)
        dv = dot(p, dos[side], 1, 0)
        dkv[a, 0, part] += dk[:half]
        dkv[b, 0, part] += dk[half:]
        dkv[a, 1, part] += dv[:half]
        dkv[b, 1, part] += dv[half:]

    def run(job, masked):
        @pl.loop(0, blocks)
        def _(t):
            job(t, 1, 0, 2 * t, 2 * t + 1, *((None,) if masked else ()))

        @pl.loop(0, blocks + 1)
        def _(t):
            side, part, a, b, limit = partial_job(t)
            job(t + blocks, side, part, a, b, *((limit,) if masked else ()))

    run(score_job, True)
    run(prob_job, False)
    for side in range(2):
        inverse = 1.0 / total[side]
        o = acc[side] * inverse
        g = jnp.transpose(dos[side].astype(jnp.float32))
        total[side] = jnp.sum(o * g, axis=0, keepdims=True) * inverse
        dos[side] = jnp.transpose(g * inverse).astype(jnp.bfloat16)
        o = jnp.transpose(o)
        o_ref[0, side * half:(side + 1) * half, :] = jnp.where(
            first, o[:half], o[half:]).astype(o_ref.dtype)
    acc[...] = jnp.zeros(acc.shape, jnp.float32)
    run(back_job, False)
    for side in range(2):
        dq = jnp.transpose(acc[side] * (1.0 / math.sqrt(HEAD_SIZE)))
        dq_ref[0, side * half:(side + 1) * half, :] = jnp.where(
            first, dq[:half], dq[half:]).astype(dq_ref.dtype)
    dkv_ref[:, :, 0] = dkv[...].astype(dkv_ref.dtype)


def attention(queries, grads, keys_values):
    seqs, rows, width = queries.shape
    members = keys_values.shape[0]
    half = rows // 2
    both = 2 * half
    keys_values = keys_values.reshape(members, 2, seqs, 2, half, width)
    row_spec = pl.BlockSpec((1, rows, PAIR), lambda s, p: (s, 0, p))
    kv_spec = pl.BlockSpec((members, 2, 1, 2, half, PAIR), lambda s, p: (0, 0, s, 0, 0, p))
    jobs = members + 1
    work = seqs * (width // PAIR) * jobs * both * both * PAIR * 2
    out = pl.pallas_call(
        lambda *refs: attention_kernel(members, half, *refs),
        grid=(seqs, width // PAIR),
        in_specs=[row_spec, row_spec, kv_spec],
        out_specs=[row_spec, row_spec, kv_spec],
        out_shape=[
            jax.ShapeDtypeStruct(queries.shape, jnp.bfloat16),
            jax.ShapeDtypeStruct(queries.shape, jnp.float32),
            jax.ShapeDtypeStruct(keys_values.shape, jnp.bfloat16),
        ],
        scratch_shapes=[
            pltpu.VMEM((2, both, PAIR), jnp.bfloat16),
            pltpu.VMEM((2, both, PAIR), jnp.bfloat16),
            pltpu.VMEM((jobs, both, both), jnp.float32),
            pltpu.VMEM((jobs, both, both), jnp.bfloat16),
            pltpu.VMEM((both, both), jnp.int32),
            pltpu.VMEM((2, 1, both), jnp.float32),
            pltpu.VMEM((2, 1, both), jnp.float32),
            pltpu.VMEM((2, PAIR, both), jnp.float32),
            pltpu.VMEM((members, 2, 2, half, PAIR), jnp.float32),
        ],
        compiler_params=pltpu.CompilerParams(vmem_limit_bytes=50 * 1024 * 1024),
        cost_estimate=pl.CostEstimate(
            flops=work * 6,
            bytes_accessed=2 * 2 * keys_values.size + 8 * queries.size,
            transcendentals=seqs * (width // PAIR) * jobs * both * both,
        ),
    )(queries, grads, keys_values)
    return out[0], out[1], out[2].reshape(members, 2, seqs, rows, width)


def rotate(values, cosine, sine_table):
    half_dim = ROT // 2
    leading = values[..., :half_dim]
    trailing = values[..., half_dim:ROT]
    return jnp.concatenate(
        [
            leading * cosine - trailing * sine_table,
            trailing * cosine + leading * sine_table,
            values[..., ROT:],
        ],
        axis=-1,
    )


def arranged_position(member, within, block_rows, members):
    half_rows = block_rows // 2
    return jnp.where(
        within < half_rows,
        member * half_rows + within,
        (2 * members - 1 - member) * half_rows + within - half_rows,
    )


def mm(a, b, ca, cb):
    return lax.dot_general(a, b, (((ca,), (cb,)), ((), ())), preferred_element_type=jnp.float32)


def per_device(
    layer_input,
    attention_gain,
    attention_shift,
    query_key_value_weight,
    query_key_value_bias,
    attention_output_weight,
    output_bias,
    feed_gain,
    feed_shift,
    up_projection_weight,
    up_projection_bias,
    down_projection_weight,
    down_bias,
    cotangent,
):
    f32, bf16 = jnp.float32, jnp.bfloat16
    seqs, rows, model = layer_input.shape
    tokens = seqs * rows
    parts = lax.axis_size("fsdp")
    members = lax.axis_size("context")
    member = lax.axis_index("context")
    share = model // parts
    width = query_key_value_weight.shape[2]
    heads = width // HEAD_SIZE
    hidden_width = up_projection_weight.shape[1]

    small = [
        attention_gain, attention_shift, query_key_value_bias, output_bias,
        feed_gain, feed_shift, up_projection_bias, down_bias,
    ]
    packed = lax.all_gather(jnp.concatenate([v.reshape(-1) for v in small]), "fsdp", axis=0)
    whole = []
    start = 0
    for v in small:
        piece = packed[:, start:start + v.size].astype(f32).reshape((parts,) + v.shape)
        start += v.size
        whole.append(jnp.moveaxis(piece, 0, -2).reshape(v.shape[:-1] + (parts * v.shape[-1],)))
    gain_a, shift_a, heads_bias, bias_o, gain_f, shift_f, up_bias, bias_d = whole
    heads_weight = lax.all_gather(query_key_value_weight, "fsdp", axis=0, tiled=True)
    heads_weight = heads_weight.reshape(model, 3 * width)
    up_weight = lax.all_gather(up_projection_weight, "fsdp", axis=0, tiled=True)
    down_weight = lax.all_gather(down_projection_weight, "fsdp", axis=1, tiled=True)
    output_weight = lax.all_gather(attention_output_weight, "fsdp", axis=1, tiled=True)

    place = arranged_position(member, jnp.arange(rows, dtype=jnp.int32), rows, members)
    frequency = jnp.power(
        jnp.float32(rotary_base), -2.0 * jnp.arange(ROT // 2, dtype=f32) / ROT
    )
    phases = place.astype(f32)[:, None] * frequency[None, :]
    cosine = jnp.cos(phases)[:, None, :]
    sine = jnp.sin(phases)[:, None, :]

    x = layer_input.astype(f32).reshape(tokens, model)
    dy_bf = cotangent.reshape(tokens, model)
    dy = dy_bf.astype(f32)
    center = x - jnp.mean(x, axis=-1, keepdims=True)
    scale = lax.rsqrt(jnp.mean(center * center, axis=-1, keepdims=True) + norm_eps)
    xhat = center * scale
    normed_a = (xhat * gain_a + shift_a).astype(bf16)
    normed_f = (xhat * gain_f + shift_f).astype(bf16)

    projected = mm(normed_a, heads_weight, 1, 0) + heads_bias.reshape(-1)
    projected = projected.reshape(seqs, rows, 3, width)
    head_shape = (seqs, rows, heads, HEAD_SIZE)
    queries = rotate(projected[:, :, 0].reshape(head_shape), cosine, sine).astype(bf16)
    keys = rotate(projected[:, :, 1].reshape(head_shape), cosine, sine).astype(bf16)
    flat = (seqs, rows, width)
    keys_values = jnp.stack([keys.reshape(flat), projected[:, :, 2].astype(bf16)])
    keys_values = lax.all_gather(keys_values, "context", axis=0)
    queries = queries.reshape(flat) * jnp.bfloat16(1.0 / math.sqrt(HEAD_SIZE))

    hidden = mm(normed_f, up_weight, 1, 0) + up_bias.reshape(-1)
    gelu_output, gelu_back = jax.vjp(lambda t: jax.nn.gelu(t, approximate=False), hidden)
    activated = gelu_output.astype(bf16)
    feed_terms = mm(activated, down_weight, 1, 0)
    hidden_grad = gelu_back(mm(dy_bf, down_weight, 1, 1))[0].astype(bf16)
    down_grad = mm(activated, dy_bf, 0, 0)
    up_grad = mm(normed_f, hidden_grad, 0, 0)
    up_bias_grad = jnp.sum(hidden_grad.astype(f32), axis=0)
    feed_part = mm(hidden_grad, up_weight, 1, 1)

    attended_grad = mm(dy_bf, output_weight, 1, 1).astype(bf16).reshape(flat)
    attended, query_grad, kv_grad = attention(queries, attended_grad, keys_values)
    own = lax.psum_scatter(kv_grad, "context", scatter_dimension=0, tiled=True)[0]

    attended = attended.reshape(tokens, width)
    terms = mm(attended, output_weight, 1, 0) + feed_terms
    branches = lax.psum(terms.astype(bf16), "tensor").astype(f32)
    layer_output = (x + branches + bias_o + bias_d).astype(bf16)
    output_grad = mm(attended, dy_bf, 0, 0)

    query_back = rotate(query_grad.reshape(head_shape), cosine, -sine)
    key_back = rotate(own[0].astype(f32).reshape(head_shape), cosine, -sine)
    projected_grad = jnp.concatenate(
        [query_back.reshape(flat).astype(bf16), key_back.reshape(flat).astype(bf16), own[1]],
        axis=-1,
    ).reshape(tokens, 3 * width)
    heads_grad = mm(normed_a, projected_grad, 0, 0)
    heads_bias_grad = jnp.sum(projected_grad.astype(f32), axis=0)
    heads_part = mm(projected_grad, heads_weight, 1, 1)

    combined = lax.psum((heads_part * gain_a + feed_part * gain_f).astype(bf16), "tensor")
    combined = combined.astype(f32)
    input_grad = dy + scale * (
        combined
        - jnp.mean(combined, axis=-1, keepdims=True)
        - xhat * jnp.mean(combined * xhat, axis=-1, keepdims=True)
    )

    def reduce_columns(grad):
        grad = lax.psum_scatter(grad.astype(bf16), "fsdp", scatter_dimension=1, tiled=True)
        return lax.psum(grad, "context").astype(f32)

    def reduce_rows(grad):
        grad = lax.psum_scatter(grad.astype(bf16), "fsdp", scatter_dimension=0, tiled=True)
        return lax.psum(grad, "context").astype(f32)

    up_out = reduce_rows(up_grad)
    down_out = reduce_columns(down_grad)
    output_out = reduce_columns(output_grad)
    heads_out = reduce_rows(heads_grad).reshape(share, 3, width)

    def by_part(v):
        v = v.reshape(v.shape[:-1] + (parts, v.shape[-1] // parts))
        return jnp.moveaxis(v, -2, 0).reshape(parts, -1)

    shared = jnp.concatenate([by_part(v) for v in (
        jnp.sum(heads_part * xhat, axis=0), jnp.sum(heads_part, axis=0),
        jnp.sum(feed_part * xhat, axis=0), jnp.sum(feed_part, axis=0))], axis=1)
    single = jnp.concatenate([by_part(v) for v in (
        jnp.sum(dy, axis=0), heads_bias_grad.reshape(3, heads, HEAD_SIZE),
        up_bias_grad.reshape(-1, HEAD_SIZE))], axis=1)
    shared = lax.psum(shared, "tensor")
    vectors = lax.psum_scatter(
        jnp.concatenate([shared, single], axis=1), "fsdp", scatter_dimension=0, tiled=True)
    vectors = lax.psum(vectors, "context")[0]
    sizes = [share] * 5 + [3 * heads * HEAD_SIZE // parts, hidden_width // parts]
    pieces = []
    start = 0
    for size in sizes:
        pieces.append(vectors[start:start + size])
        start += size
    return (
        layer_output.reshape(seqs, rows, model),
        input_grad.reshape(seqs, rows, model),
        pieces[0],
        pieces[1],
        heads_out,
        pieces[5].reshape(query_key_value_bias.shape),
        output_out,
        pieces[4],
        pieces[2],
        pieces[3],
        up_out,
        pieces[6].reshape(up_projection_bias.shape),
        down_out,
        pieces[4],
    )


def solution(mesh):
    in_specs = (
        P("fsdp", "context", None),
        P("fsdp"),
        P("fsdp"),
        P("fsdp", None, "tensor"),
        P(None, "tensor", "fsdp"),
        P("tensor", "fsdp"),
        P("fsdp"),
        P("fsdp"),
        P("fsdp"),
        P("fsdp", "tensor"),
        P("tensor", "fsdp"),
        P("tensor", "fsdp"),
        P("fsdp"),
        P("fsdp", "context", None),
    )
    out_specs = (
        P("fsdp", "context", None),
        P("fsdp", "context", None),
        P("fsdp"),
        P("fsdp"),
        P("fsdp", None, "tensor"),
        P(None, "tensor", "fsdp"),
        P("tensor", "fsdp"),
        P("fsdp"),
        P("fsdp"),
        P("fsdp"),
        P("fsdp", "tensor"),
        P("tensor", "fsdp"),
        P("tensor", "fsdp"),
        P("fsdp"),
    )
    return jax.shard_map(
        per_device, mesh=mesh, in_specs=in_specs, out_specs=out_specs, check_vma=False
    )
```

```python
import math

import jax
import jax.numpy as jnp
from jax import lax
from jax.experimental import pallas as pl
from jax.experimental.pallas import tpu as pltpu
from jax.sharding import PartitionSpec as P

HEAD_SIZE = 64
ROT = 16
PAIR = 2 * HEAD_SIZE


norm_eps = 1e-05
rotary_base = 10000.0
masked_score = -1e30


def dot(a, b, ca, cb):
    return lax.dot_general(a, b, (((ca,), (cb,)), ((), ())), preferred_element_type=jnp.float32)


def attention_kernel(
    members, half, q_ref, do_ref, kv_ref, o_ref, dq_ref, dkv_ref,
    qs, dos, scores, probs, offsets, top, total, acc, dkv
):
    both = 2 * half
    blocks = members // 2
    member = lax.axis_index("context")
    lane = lax.broadcasted_iota(jnp.int32, (half, PAIR), 1)
    first = lane < HEAD_SIZE
    zero = jnp.zeros((half, PAIR), jnp.bfloat16)
    for side in range(2):
        q = q_ref[0, side * half:(side + 1) * half, :]
        g = do_ref[0, side * half:(side + 1) * half, :]
        qs[side, 0:half, :] = jnp.where(first, q, zero)
        qs[side, half:both, :] = jnp.where(first, zero, q)
        dos[side, 0:half, :] = jnp.where(first, g, zero)
        dos[side, half:both, :] = jnp.where(first, zero, g)
    row = lax.broadcasted_iota(jnp.int32, (both, both), 0)
    column = lax.broadcasted_iota(jnp.int32, (both, both), 1)
    offsets[...] = row - jnp.where(column >= half, column - half, column)
    top[...] = jnp.full(top.shape, masked_score, jnp.float32)
    total[...] = jnp.zeros(total.shape, jnp.float32)
    acc[...] = jnp.zeros(acc.shape, jnp.float32)
    dkv[...] = jnp.zeros(dkv.shape, jnp.float32)

    low_jobs = (member + 2) // 2
    jobs = 2 * blocks + 1

    def partial_job(t):
        low = t < low_jobs
        block = jnp.where(low, t, t - low_jobs)
        side = jnp.where(low, 0, 1)
        query_base = jnp.where(low, member, 2 * members - 1 - member) * half
        key_base = jnp.where(low, 0, members * half) + block * both
        first_member = jnp.where(low, 2 * block, members - 1 - 2 * block)
        second_member = jnp.where(low, 2 * block + 1, members - 2 - 2 * block)
        return side, side, first_member, second_member, query_base - key_base

    def load(which, part, a, b):
        return jnp.concatenate([kv_ref[a, which, 0, part], kv_ref[b, which, 0, part]], axis=0)

    def score_job(t, side, part, a, b, limit):
        s = dot(load(0, part, a, b), qs[side], 1, 1)
        if limit is not None:
            s = jnp.where(offsets[...] <= limit, s, masked_score)
        scores[t] = s
        top[side] = jnp.maximum(top[side], jnp.max(s, axis=0, keepdims=True))

    def prob_job(t, side, part, a, b):
        p = jnp.exp(scores[t] - top[side])
        total[side] += jnp.sum(p, axis=0, keepdims=True)
        p = p.astype(jnp.bfloat16)
        probs[t] = p
        acc[side] += dot(load(1, part, a, b), p, 0, 0)

    def back_job(t, side, part, a, b):
        p = probs[t]
        k = load(0, part, a, b)
        dp = dot(load(1, part, a, b), dos[side], 1, 1)
        ds = (p.astype(jnp.float32) * (dp - total[side])).astype(jnp.bfloat16)
        acc[side] += dot(k, ds, 0, 0)
        dk = dot(ds, qs[side], 1, 0)
        dv = dot(p, dos[side], 1, 0)
        dkv[a, 0, part] += dk[:half]
        dkv[b, 0, part] += dk[half:]
        dkv[a, 1, part] += dv[:half]
        dkv[b, 1, part] += dv[half:]

    def run(job, masked):
        @pl.loop(0, blocks)
        def _(t):
            job(t, 1, 0, 2 * t, 2 * t + 1, *((None,) if masked else ()))

        @pl.loop(0, blocks + 1)
        def _(t):
            side, part, a, b, limit = partial_job(t)
            job(t + blocks, side, part, a, b, *((limit,) if masked else ()))

    run(score_job, True)
    run(prob_job, False)
    for side in range(2):
        inverse = 1.0 / total[side]
        o = acc[side] * inverse
        g = jnp.transpose(dos[side].astype(jnp.float32))
        total[side] = jnp.sum(o * g, axis=0, keepdims=True) * inverse
        dos[side] = jnp.transpose(g * inverse).astype(jnp.bfloat16)
        o = jnp.transpose(o)
        o_ref[0, side * half:(side + 1) * half, :] = jnp.where(
            first, o[:half], o[half:]).astype(o_ref.dtype)
    acc[...] = jnp.zeros(acc.shape, jnp.float32)
    run(back_job, False)
    for side in range(2):
        dq = jnp.transpose(acc[side] * (1.0 / math.sqrt(HEAD_SIZE)))
        dq_ref[0, side * half:(side + 1) * half, :] = jnp.where(
            first, dq[:half], dq[half:]).astype(dq_ref.dtype)
    dkv_ref[:, :, 0] = dkv[...].astype(dkv_ref.dtype)


def attention(queries, grads, keys_values):
    seqs, rows, width = queries.shape
    members = keys_values.shape[0]
    half = rows // 2
    both = 2 * half
    keys_values = keys_values.reshape(members, 2, seqs, 2, half, width)
    row_spec = pl.BlockSpec((1, rows, PAIR), lambda s, p: (s, 0, p))
    kv_spec = pl.BlockSpec((members, 2, 1, 2, half, PAIR), lambda s, p: (0, 0, s, 0, 0, p))
    jobs = members + 1
    work = seqs * (width // PAIR) * jobs * both * both * PAIR * 2
    out = pl.pallas_call(
        lambda *refs: attention_kernel(members, half, *refs),
        grid=(seqs, width // PAIR),
        in_specs=[row_spec, row_spec, kv_spec],
        out_specs=[row_spec, row_spec, kv_spec],
        out_shape=[
            jax.ShapeDtypeStruct(queries.shape, jnp.bfloat16),
            jax.ShapeDtypeStruct(queries.shape, jnp.float32),
            jax.ShapeDtypeStruct(keys_values.shape, jnp.bfloat16),
        ],
        scratch_shapes=[
            pltpu.VMEM((2, both, PAIR), jnp.bfloat16),
            pltpu.VMEM((2, both, PAIR), jnp.bfloat16),
            pltpu.VMEM((jobs, both, both), jnp.float32),
            pltpu.VMEM((jobs, both, both), jnp.bfloat16),
            pltpu.VMEM((both, both), jnp.int32),
            pltpu.VMEM((2, 1, both), jnp.float32),
            pltpu.VMEM((2, 1, both), jnp.float32),
            pltpu.VMEM((2, PAIR, both), jnp.float32),
            pltpu.VMEM((members, 2, 2, half, PAIR), jnp.float32),
        ],
        compiler_params=pltpu.CompilerParams(vmem_limit_bytes=50 * 1024 * 1024),
        cost_estimate=pl.CostEstimate(
            flops=work * 6,
            bytes_accessed=2 * 2 * keys_values.size + 8 * queries.size,
            transcendentals=seqs * (width // PAIR) * jobs * both * both,
        ),
    )(queries, grads, keys_values)
    return out[0], out[1], out[2].reshape(members, 2, seqs, rows, width)


def rotate(values, even, ahead, behind):
    half_dim = ROT // 2
    return (
        values * even
        + jnp.roll(values, -half_dim, axis=-1) * ahead
        + jnp.roll(values, half_dim, axis=-1) * behind
    )


def swap(value, axis):
    return lax.ppermute(value, axis, [(0, 1), (1, 0)])


def sibling(value):
    count = lax.axis_size("context")
    return lax.ppermute(value, "context", [(i, i ^ 1) for i in range(count)])


def whole_weight(shard, axis):
    if lax.axis_size("fsdp") != 2:
        return lax.all_gather(shard, "fsdp", axis=axis, tiled=True)
    core = lax.axis_index("context") % 2
    rows = shard.shape[0] // 2
    mine = swap(lax.dynamic_slice_in_dim(shard, core * rows, rows, 0), "fsdp")
    theirs = sibling(mine)
    first = jnp.where(core == 0, mine, theirs)
    second = jnp.where(core == 0, theirs, mine)
    far = jnp.concatenate([first, second], axis=0)
    left = lax.axis_index("fsdp") == 0
    return jnp.concatenate([jnp.where(left, shard, far), jnp.where(left, far, shard)], axis=axis)


def sum_pair(value):
    if lax.axis_size("tensor") != 2:
        return lax.psum(value, "tensor").astype(jnp.float32)
    return value.astype(jnp.float32) + swap(value, "tensor").astype(jnp.float32)


def reduce_gradient(grad, order):
    f32, bf16 = jnp.float32, jnp.bfloat16
    parts = lax.axis_size("fsdp")
    members = lax.axis_size("context")
    if parts != 2:
        grad = lax.psum_scatter(grad.astype(bf16), "fsdp", scatter_dimension=0, tiled=True)
        return lax.psum(grad, "context")
    core = lax.axis_index("context") % 2
    side = lax.axis_index("fsdp")
    model, columns = grad.shape
    grad = grad.astype(bf16).reshape(2, 2, model // 4, columns)
    away = lax.dynamic_slice_in_dim(grad, 1 - core, 1, 1)
    kept = lax.dynamic_slice_in_dim(grad, core, 1, 1)
    grad = (kept.astype(f32) + sibling(away).astype(f32)).astype(bf16)[:, 0]
    away = lax.dynamic_slice_in_dim(grad, 1 - side, 1, 0)
    kept = lax.dynamic_slice_in_dim(grad, side, 1, 0)
    grad = (kept.astype(f32) + swap(away, "fsdp").astype(f32)).astype(bf16)[0]
    groups = [list(range(c, members, 2)) for c in order]
    grad = lax.psum(grad, "context", axis_index_groups=groups)
    theirs = sibling(grad)
    return jnp.concatenate(
        [jnp.where(core == 0, grad, theirs), jnp.where(core == 0, theirs, grad)], axis=0)


def arranged_position(member, within, block_rows, members):
    half_rows = block_rows // 2
    return jnp.where(
        within < half_rows,
        member * half_rows + within,
        (2 * members - 1 - member) * half_rows + within - half_rows,
    )


def mm(a, b, ca, cb):
    return lax.dot_general(a, b, (((ca,), (cb,)), ((), ())), preferred_element_type=jnp.float32)


def per_device(
    layer_input,
    attention_gain,
    attention_shift,
    query_key_value_weight,
    query_key_value_bias,
    attention_output_weight,
    output_bias,
    feed_gain,
    feed_shift,
    up_projection_weight,
    up_projection_bias,
    down_projection_weight,
    down_bias,
    cotangent,
):
    f32, bf16 = jnp.float32, jnp.bfloat16
    seqs, rows, model = layer_input.shape
    tokens = seqs * rows
    parts = lax.axis_size("fsdp")
    members = lax.axis_size("context")
    member = lax.axis_index("context")
    share = model // parts
    width = query_key_value_weight.shape[2]
    heads = width // HEAD_SIZE
    hidden_width = up_projection_weight.shape[1]

    small = [
        attention_gain, attention_shift, query_key_value_bias, output_bias,
        feed_gain, feed_shift, up_projection_bias, down_bias,
    ]
    packed = lax.all_gather(jnp.concatenate([v.reshape(-1) for v in small]), "fsdp", axis=0)
    whole = []
    start = 0
    for v in small:
        piece = packed[:, start:start + v.size].astype(f32).reshape((parts,) + v.shape)
        start += v.size
        whole.append(jnp.moveaxis(piece, 0, -2).reshape(v.shape[:-1] + (parts * v.shape[-1],)))
    gain_a, shift_a, heads_bias, bias_o, gain_f, shift_f, up_bias, bias_d = whole
    heads_weight = whole_weight(query_key_value_weight.reshape(share, 3 * width), 0)
    up_weight = whole_weight(up_projection_weight, 0)
    output_weight = whole_weight(attention_output_weight, 1)
    down_weight = whole_weight(down_projection_weight, 1)

    place = arranged_position(member, jnp.arange(rows, dtype=jnp.int32), rows, members)
    frequency = jnp.power(
        jnp.float32(rotary_base), -2.0 * jnp.arange(ROT // 2, dtype=f32) / ROT
    )
    phases = place.astype(f32)[:, None] * frequency[None, :]
    cosine, sine = jnp.cos(phases), jnp.sin(phases)
    rest = HEAD_SIZE - ROT
    none = jnp.zeros((rows, ROT // 2), f32)
    blank = jnp.zeros((rows, rest), f32)
    even = jnp.concatenate([cosine, cosine, jnp.ones((rows, rest), f32)], axis=1)
    even = jnp.tile(even, (1, heads))[None]
    ahead = jnp.tile(jnp.concatenate([-sine, none, blank], axis=1), (1, heads))[None]
    behind = jnp.tile(jnp.concatenate([none, sine, blank], axis=1), (1, heads))[None]

    x = layer_input.astype(f32).reshape(tokens, model)
    dy_bf = cotangent.reshape(tokens, model)
    dy = dy_bf.astype(f32)
    center = x - jnp.mean(x, axis=-1, keepdims=True)
    scale = lax.rsqrt(jnp.mean(center * center, axis=-1, keepdims=True) + norm_eps)
    xhat = center * scale
    normed_a = (xhat * gain_a + shift_a).astype(bf16)
    normed_f = (xhat * gain_f + shift_f).astype(bf16)

    projected = mm(normed_a, heads_weight, 1, 0) + heads_bias.reshape(-1)
    flat = (seqs, rows, width)
    queries, keys, values = (
        projected[:, i * width:(i + 1) * width].reshape(flat) for i in range(3))
    queries = rotate(queries, even, ahead, behind).astype(bf16)
    keys = rotate(keys, even, ahead, behind).astype(bf16)
    keys_values = jnp.stack([keys, values.astype(bf16)])
    keys_values = lax.all_gather(keys_values, "context", axis=0)
    queries = queries * jnp.bfloat16(1.0 / math.sqrt(HEAD_SIZE))

    hidden = mm(normed_f, up_weight, 1, 0) + up_bias.reshape(-1)
    gelu_output, gelu_back = jax.vjp(lambda t: jax.nn.gelu(t, approximate=False), hidden)
    activated = gelu_output.astype(bf16)
    feed_terms = mm(activated, down_weight, 1, 0)
    hidden_grad = gelu_back(mm(dy_bf, down_weight, 1, 1))[0].astype(bf16)
    down_grad = mm(dy_bf, activated, 0, 0)
    up_grad = mm(normed_f, hidden_grad, 0, 0)
    up_bias_grad = jnp.sum(hidden_grad.astype(f32), axis=0)
    feed_part = mm(hidden_grad, up_weight, 1, 1)

    attended_grad = mm(dy_bf, output_weight, 1, 1).astype(bf16).reshape(flat)
    attended, query_grad, kv_grad = attention(queries, attended_grad, keys_values)
    own = lax.psum_scatter(kv_grad, "context", scatter_dimension=0, tiled=True)[0]

    attended = attended.reshape(tokens, width)
    terms = mm(attended, output_weight, 1, 0) + feed_terms
    branches = sum_pair(terms.astype(bf16))
    layer_output = (x + branches + bias_o + bias_d).astype(bf16)
    output_grad = mm(dy_bf, attended, 0, 0)

    query_back = rotate(query_grad, even, -ahead, -behind)
    key_back = rotate(own[0].astype(f32), even, -ahead, -behind)
    projected_grad = jnp.concatenate(
        [query_back.astype(bf16), key_back.astype(bf16), own[1]],
        axis=-1,
    ).reshape(tokens, 3 * width)
    heads_grad = mm(normed_a, projected_grad, 0, 0)
    heads_bias_grad = jnp.sum(projected_grad.astype(f32), axis=0)
    heads_part = mm(projected_grad, heads_weight, 1, 1)

    combined = sum_pair((heads_part * gain_a + feed_part * gain_f).astype(bf16))
    input_grad = dy + scale * (
        combined
        - jnp.mean(combined, axis=-1, keepdims=True)
        - xhat * jnp.mean(combined * xhat, axis=-1, keepdims=True)
    )

    def as_columns(vectors):
        flats = []
        for v in vectors:
            v = v.reshape(v.shape[:-1] + (parts, v.shape[-1] // parts))
            flats.append(jnp.moveaxis(v, -2, 0).reshape(parts, -1))
        flat_all = jnp.concatenate(flats, axis=1)
        columns = -(-flat_all.shape[1] // share)
        flat_all = jnp.pad(flat_all, ((0, 0), (0, columns * share - flat_all.shape[1])))
        return jnp.moveaxis(flat_all.reshape(parts, columns, share), 1, 2).reshape(
            model, columns)

    def vectors_of(columns, sizes):
        flat_all = columns.astype(f32).T.reshape(-1)
        out, start = [], 0
        for size in sizes:
            out.append(flat_all[start:start + size])
            start += size
        return out

    def sum_tensor(v):
        return lax.psum(v, "tensor") if lax.axis_size("tensor") != 2 else v + swap(v, "tensor")

    feed_sums = sum_tensor(jnp.stack([jnp.sum(feed_part * xhat, axis=0), jnp.sum(feed_part, axis=0)]))
    early = as_columns([
        feed_sums[0], feed_sums[1], jnp.sum(dy, axis=0), up_bias_grad.reshape(-1, HEAD_SIZE)])
    early = reduce_gradient(jnp.concatenate([up_grad, down_grad, early], axis=1), (0, 1))
    up_out = early[:, :hidden_width].astype(f32)
    down_out = early[:, hidden_width:2 * hidden_width].astype(f32).T
    gain_f_out, shift_f_out, bias_out, up_bias_out = vectors_of(
        early[:, 2 * hidden_width:], [share] * 3 + [hidden_width // parts])

    head_sums = sum_tensor(
        jnp.stack([jnp.sum(heads_part * xhat, axis=0), jnp.sum(heads_part, axis=0)]))
    late = as_columns([
        head_sums[0], head_sums[1], heads_bias_grad.reshape(3, heads, HEAD_SIZE)])
    late = reduce_gradient(
        jnp.concatenate([heads_grad, output_grad, late], axis=1), (1, 0))
    heads_out = late[:, :3 * width].astype(f32).reshape(share, 3, width)
    output_out = late[:, 3 * width:4 * width].astype(f32).T
    gain_a_out, shift_a_out, heads_bias_out = vectors_of(
        late[:, 4 * width:], [share] * 2 + [3 * width // parts])
    return (
        layer_output.reshape(seqs, rows, model),
        input_grad.reshape(seqs, rows, model),
        gain_a_out,
        shift_a_out,
        heads_out,
        heads_bias_out.reshape(query_key_value_bias.shape),
        output_out,
        bias_out,
        gain_f_out,
        shift_f_out,
        up_out,
        up_bias_out.reshape(up_projection_bias.shape),
        down_out,
        bias_out,
    )


def solution(mesh):
    in_specs = (
        P("fsdp", "context", None),
        P("fsdp"),
        P("fsdp"),
        P("fsdp", None, "tensor"),
        P(None, "tensor", "fsdp"),
        P("tensor", "fsdp"),
        P("fsdp"),
        P("fsdp"),
        P("fsdp"),
        P("fsdp", "tensor"),
        P("tensor", "fsdp"),
        P("tensor", "fsdp"),
        P("fsdp"),
        P("fsdp", "context", None),
    )
    out_specs = (
        P("fsdp", "context", None),
        P("fsdp", "context", None),
        P("fsdp"),
        P("fsdp"),
        P("fsdp", None, "tensor"),
        P(None, "tensor", "fsdp"),
        P("tensor", "fsdp"),
        P("fsdp"),
        P("fsdp"),
        P("fsdp"),
        P("fsdp", "tensor"),
        P("tensor", "fsdp"),
        P("tensor", "fsdp"),
        P("fsdp"),
    )
    return jax.shard_map(
        per_device, mesh=mesh, in_specs=in_specs, out_specs=out_specs, check_vma=False
    )
```

```python
import math

import jax
import jax.numpy as jnp
from jax import lax
from jax.experimental import pallas as pl
from jax.experimental.pallas import tpu as pltpu
from jax.sharding import PartitionSpec as P

HEAD_SIZE = 64
ROT = 16
PAIR = 2 * HEAD_SIZE


norm_eps = 1e-05
rotary_base = 10000.0
masked_score = -1e30


def dot(a, b, ca, cb):
    return lax.dot_general(a, b, (((ca,), (cb,)), ((), ())), preferred_element_type=jnp.float32)


def attention_kernel(
    members, half, q_ref, do_ref, kv_ref, after_ref, o_ref, dq_ref, dkv_ref,
    qs, dos, scores, probs, offsets, top, total, acc, dkv
):
    both = 2 * half
    blocks = members // 2
    member = lax.axis_index("context")
    lane = lax.broadcasted_iota(jnp.int32, (half, PAIR), 1)
    first = lane < HEAD_SIZE
    zero = jnp.zeros((half, PAIR), jnp.bfloat16)
    for side in range(2):
        q = q_ref[0, side * half:(side + 1) * half, :]
        g = do_ref[0, side * half:(side + 1) * half, :]
        qs[side, 0:half, :] = jnp.where(first, q, zero)
        qs[side, half:both, :] = jnp.where(first, zero, q)
        dos[side, 0:half, :] = jnp.where(first, g, zero)
        dos[side, half:both, :] = jnp.where(first, zero, g)
    row = lax.broadcasted_iota(jnp.int32, (both, both), 0)
    column = lax.broadcasted_iota(jnp.int32, (both, both), 1)
    offsets[...] = row - jnp.where(column >= half, column - half, column)
    top[...] = jnp.full(top.shape, masked_score, jnp.float32)
    total[...] = jnp.zeros(total.shape, jnp.float32)
    acc[...] = jnp.zeros(acc.shape, jnp.float32)
    dkv[...] = jnp.zeros(dkv.shape, jnp.float32)

    low_jobs = (member + 2) // 2
    jobs = 2 * blocks + 1

    def partial_job(t):
        low = t < low_jobs
        block = jnp.where(low, t, t - low_jobs)
        side = jnp.where(low, 0, 1)
        query_base = jnp.where(low, member, 2 * members - 1 - member) * half
        key_base = jnp.where(low, 0, members * half) + block * both
        first_member = jnp.where(low, 2 * block, members - 1 - 2 * block)
        second_member = jnp.where(low, 2 * block + 1, members - 2 - 2 * block)
        return side, side, first_member, second_member, query_base - key_base

    def load(which, part, a, b):
        return jnp.concatenate([kv_ref[a, which, 0, part], kv_ref[b, which, 0, part]], axis=0)

    def score_job(t, side, part, a, b, limit):
        s = dot(load(0, part, a, b), qs[side], 1, 1)
        if limit is not None:
            s = jnp.where(offsets[...] <= limit, s, masked_score)
        scores[t] = s
        top[side] = jnp.maximum(top[side], jnp.max(s, axis=0, keepdims=True))

    def prob_job(t, side, part, a, b):
        p = jnp.exp(scores[t] - top[side])
        total[side] += jnp.sum(p, axis=0, keepdims=True)
        p = p.astype(jnp.bfloat16)
        probs[t] = p
        acc[side] += dot(load(1, part, a, b), p, 0, 0)

    def back_job(t, side, part, a, b):
        p = probs[t]
        k = load(0, part, a, b)
        dp = dot(load(1, part, a, b), dos[side], 1, 1)
        ds = (p.astype(jnp.float32) * (dp - total[side])).astype(jnp.bfloat16)
        acc[side] += dot(k, ds, 0, 0)
        dk = dot(ds, qs[side], 1, 0)
        dv = dot(p, dos[side], 1, 0)
        dkv[a, 0, part] += dk[:half]
        dkv[b, 0, part] += dk[half:]
        dkv[a, 1, part] += dv[:half]
        dkv[b, 1, part] += dv[half:]

    def run(job, masked):
        @pl.loop(0, blocks)
        def _(t):
            job(t, 1, 0, 2 * t, 2 * t + 1, *((None,) if masked else ()))

        @pl.loop(0, blocks + 1)
        def _(t):
            side, part, a, b, limit = partial_job(t)
            job(t + blocks, side, part, a, b, *((limit,) if masked else ()))

    run(score_job, True)
    run(prob_job, False)
    for side in range(2):
        inverse = 1.0 / total[side]
        o = acc[side] * inverse
        g = jnp.transpose(dos[side].astype(jnp.float32))
        total[side] = jnp.sum(o * g, axis=0, keepdims=True) * inverse
        dos[side] = jnp.transpose(g * inverse).astype(jnp.bfloat16)
        o = jnp.transpose(o)
        o_ref[0, side * half:(side + 1) * half, :] = jnp.where(
            first, o[:half], o[half:]).astype(o_ref.dtype)
    acc[...] = jnp.zeros(acc.shape, jnp.float32)
    run(back_job, False)
    for side in range(2):
        dq = jnp.transpose(acc[side] * (1.0 / math.sqrt(HEAD_SIZE)))
        dq_ref[0, side * half:(side + 1) * half, :] = jnp.where(
            first, dq[:half], dq[half:]).astype(dq_ref.dtype)
    dkv_ref[:, :, 0] = dkv[...].astype(dkv_ref.dtype)


def attention(queries, grads, keys_values, after):
    seqs, rows, width = queries.shape
    members = keys_values.shape[0]
    half = rows // 2
    both = 2 * half
    keys_values = keys_values.reshape(members, 2, seqs, 2, half, width)
    row_spec = pl.BlockSpec((1, rows, PAIR), lambda s, p: (s, 0, p))
    kv_spec = pl.BlockSpec((members, 2, 1, 2, half, PAIR), lambda s, p: (0, 0, s, 0, 0, p))
    jobs = members + 1
    work = seqs * (width // PAIR) * jobs * both * both * PAIR * 2
    out = pl.pallas_call(
        lambda *refs: attention_kernel(members, half, *refs),
        grid=(seqs, width // PAIR),
        in_specs=[row_spec, row_spec, kv_spec, pl.BlockSpec(memory_space=pl.ANY)],
        out_specs=[row_spec, row_spec, kv_spec],
        out_shape=[
            jax.ShapeDtypeStruct(queries.shape, jnp.bfloat16),
            jax.ShapeDtypeStruct(queries.shape, jnp.float32),
            jax.ShapeDtypeStruct(keys_values.shape, jnp.bfloat16),
        ],
        scratch_shapes=[
            pltpu.VMEM((2, both, PAIR), jnp.bfloat16),
            pltpu.VMEM((2, both, PAIR), jnp.bfloat16),
            pltpu.VMEM((jobs, both, both), jnp.float32),
            pltpu.VMEM((jobs, both, both), jnp.bfloat16),
            pltpu.VMEM((both, both), jnp.int32),
            pltpu.VMEM((2, 1, both), jnp.float32),
            pltpu.VMEM((2, 1, both), jnp.float32),
            pltpu.VMEM((2, PAIR, both), jnp.float32),
            pltpu.VMEM((members, 2, 2, half, PAIR), jnp.float32),
        ],
        compiler_params=pltpu.CompilerParams(vmem_limit_bytes=50 * 1024 * 1024),
        cost_estimate=pl.CostEstimate(
            flops=work * 6,
            bytes_accessed=2 * 2 * keys_values.size + 8 * queries.size,
            transcendentals=seqs * (width // PAIR) * jobs * both * both,
        ),
    )(queries, grads, keys_values, after)
    return out[0], out[1], out[2].reshape(members, 2, seqs, rows, width)


def rotate(values, even, ahead, behind):
    half_dim = ROT // 2
    return (
        values * even
        + jnp.roll(values, -half_dim, axis=-1) * ahead
        + jnp.roll(values, half_dim, axis=-1) * behind
    )


def swap(value, axis):
    return lax.ppermute(value, axis, [(0, 1), (1, 0)])


def sibling(value):
    count = lax.axis_size("context")
    return lax.ppermute(value, "context", [(i, i ^ 1) for i in range(count)])


def whole_weight(shard, axis):
    if lax.axis_size("fsdp") != 2:
        return lax.all_gather(shard, "fsdp", axis=axis, tiled=True)
    core = lax.axis_index("context") % 2
    rows = shard.shape[0] // 2
    mine = swap(lax.dynamic_slice_in_dim(shard, core * rows, rows, 0), "fsdp")
    theirs = sibling(mine)
    first = jnp.where(core == 0, mine, theirs)
    second = jnp.where(core == 0, theirs, mine)
    far = jnp.concatenate([first, second], axis=0)
    left = lax.axis_index("fsdp") == 0
    return jnp.concatenate([jnp.where(left, shard, far), jnp.where(left, far, shard)], axis=axis)


def sum_pair(value):
    if lax.axis_size("tensor") != 2:
        return lax.psum(value, "tensor").astype(jnp.float32)
    return value.astype(jnp.float32) + swap(value, "tensor").astype(jnp.float32)


def sum_cores(grad):
    grad = grad.astype(jnp.bfloat16)
    if lax.axis_size("fsdp") != 2:
        return grad
    core = lax.axis_index("context") % 2
    model, columns = grad.shape
    grad = grad.reshape(2, 2, model // 4, columns)
    away = lax.dynamic_slice_in_dim(grad, 1 - core, 1, 1)
    kept = lax.dynamic_slice_in_dim(grad, core, 1, 1)
    total = kept.astype(jnp.float32) + sibling(away).astype(jnp.float32)
    return total.astype(jnp.bfloat16)[:, 0]


def sum_fsdp(grad):
    if lax.axis_size("fsdp") != 2:
        return lax.psum_scatter(grad, "fsdp", scatter_dimension=0, tiled=True)
    side = lax.axis_index("fsdp")
    away = lax.dynamic_slice_in_dim(grad, 1 - side, 1, 0)
    kept = lax.dynamic_slice_in_dim(grad, side, 1, 0)
    total = kept.astype(jnp.float32) + swap(away, "fsdp").astype(jnp.float32)
    return total.astype(jnp.bfloat16)[0]


def sum_context(grad, order):
    if lax.axis_size("fsdp") != 2:
        return lax.psum(grad, "context")
    members = lax.axis_size("context")
    core = lax.axis_index("context") % 2
    groups = [list(range(c, members, 2)) for c in order]
    grad = lax.psum(grad, "context", axis_index_groups=groups)
    theirs = sibling(grad)
    return jnp.concatenate(
        [jnp.where(core == 0, grad, theirs), jnp.where(core == 0, theirs, grad)], axis=0)


def arranged_position(member, within, block_rows, members):
    half_rows = block_rows // 2
    return jnp.where(
        within < half_rows,
        member * half_rows + within,
        (2 * members - 1 - member) * half_rows + within - half_rows,
    )


def mm(a, b, ca, cb):
    return lax.dot_general(a, b, (((ca,), (cb,)), ((), ())), preferred_element_type=jnp.float32)


def per_device(
    layer_input,
    attention_gain,
    attention_shift,
    query_key_value_weight,
    query_key_value_bias,
    attention_output_weight,
    output_bias,
    feed_gain,
    feed_shift,
    up_projection_weight,
    up_projection_bias,
    down_projection_weight,
    down_bias,
    cotangent,
):
    f32, bf16 = jnp.float32, jnp.bfloat16
    seqs, rows, model = layer_input.shape
    tokens = seqs * rows
    parts = lax.axis_size("fsdp")
    members = lax.axis_size("context")
    member = lax.axis_index("context")
    share = model // parts
    width = query_key_value_weight.shape[2]
    heads = width // HEAD_SIZE
    hidden_width = up_projection_weight.shape[1]

    small = [
        attention_gain, attention_shift, query_key_value_bias, output_bias,
        feed_gain, feed_shift, up_projection_bias, down_bias,
    ]
    packed = jnp.concatenate([v.reshape(-1) for v in small])
    if parts == 2:
        far, left = swap(packed, "fsdp"), lax.axis_index("fsdp") == 0
        packed = jnp.stack([jnp.where(left, packed, far), jnp.where(left, far, packed)])
    else:
        packed = lax.all_gather(packed, "fsdp", axis=0)
    whole = []
    start = 0
    for v in small:
        piece = packed[:, start:start + v.size].astype(f32).reshape((parts,) + v.shape)
        start += v.size
        whole.append(jnp.moveaxis(piece, 0, -2).reshape(v.shape[:-1] + (parts * v.shape[-1],)))
    gain_a, shift_a, heads_bias, bias_o, gain_f, shift_f, up_bias, bias_d = whole
    heads_weight = whole_weight(query_key_value_weight.reshape(share, 3 * width), 0)
    up_weight = whole_weight(up_projection_weight, 0)
    output_weight = whole_weight(attention_output_weight, 1)
    down_weight = whole_weight(down_projection_weight, 1)

    place = arranged_position(member, jnp.arange(rows, dtype=jnp.int32), rows, members)
    frequency = jnp.power(
        jnp.float32(rotary_base), -2.0 * jnp.arange(ROT // 2, dtype=f32) / ROT
    )
    phases = place.astype(f32)[:, None] * frequency[None, :]
    cosine, sine = jnp.cos(phases), jnp.sin(phases)
    rest = HEAD_SIZE - ROT
    none = jnp.zeros((rows, ROT // 2), f32)
    blank = jnp.zeros((rows, rest), f32)
    even = jnp.concatenate([cosine, cosine, jnp.ones((rows, rest), f32)], axis=1)
    even = jnp.tile(even, (1, heads))[None]
    ahead = jnp.tile(jnp.concatenate([-sine, none, blank], axis=1), (1, heads))[None]
    behind = jnp.tile(jnp.concatenate([none, sine, blank], axis=1), (1, heads))[None]

    x = layer_input.astype(f32).reshape(tokens, model)
    dy_bf = cotangent.reshape(tokens, model)
    dy = dy_bf.astype(f32)
    center = x - jnp.mean(x, axis=-1, keepdims=True)
    scale = lax.rsqrt(jnp.mean(center * center, axis=-1, keepdims=True) + norm_eps)
    xhat = center * scale
    normed_a = (xhat * gain_a + shift_a).astype(bf16)
    normed_f = (xhat * gain_f + shift_f).astype(bf16)

    projected = mm(normed_a, heads_weight, 1, 0) + heads_bias.reshape(-1)
    flat = (seqs, rows, width)
    queries, keys, values = (
        projected[:, i * width:(i + 1) * width].reshape(flat) for i in range(3))
    queries = rotate(queries, even, ahead, behind).astype(bf16)
    keys = rotate(keys, even, ahead, behind).astype(bf16)
    values = values.astype(bf16)
    gathered = [
        lax.all_gather(jnp.stack([keys[i:i + 1], values[i:i + 1]]), "context", axis=0)
        for i in range(seqs)]
    queries = queries * jnp.bfloat16(1.0 / math.sqrt(HEAD_SIZE))

    def as_columns(vectors):
        flats = []
        for v in vectors:
            v = v.reshape(v.shape[:-1] + (parts, v.shape[-1] // parts))
            flats.append(jnp.moveaxis(v, -2, 0).reshape(parts, -1))
        flat_all = jnp.concatenate(flats, axis=1)
        columns = -(-flat_all.shape[1] // share)
        flat_all = jnp.pad(flat_all, ((0, 0), (0, columns * share - flat_all.shape[1])))
        return jnp.moveaxis(flat_all.reshape(parts, columns, share), 1, 2).reshape(
            model, columns)

    def vectors_of(columns, sizes):
        flat_all = columns.astype(f32).T.reshape(-1)
        out, start = [], 0
        for size in sizes:
            out.append(flat_all[start:start + size])
            start += size
        return out

    def sum_tensor(v):
        return lax.psum(v, "tensor") if lax.axis_size("tensor") != 2 else v + swap(v, "tensor")

    hidden = mm(normed_f, up_weight, 1, 0) + up_bias.reshape(-1)
    gelu_output, gelu_back = jax.vjp(lambda t: jax.nn.gelu(t, approximate=False), hidden)
    activated = gelu_output.astype(bf16)
    feed_terms = mm(activated, down_weight, 1, 0)
    hidden_grad = gelu_back(mm(dy_bf, down_weight, 1, 1))[0].astype(bf16)
    down_grad = mm(dy_bf, activated, 0, 0)
    up_grad = mm(normed_f, hidden_grad, 0, 0)
    up_bias_grad = jnp.sum(hidden_grad.astype(f32), axis=0)
    feed_part = mm(hidden_grad, up_weight, 1, 1)

    attended_grad = mm(dy_bf, output_weight, 1, 1).astype(bf16).reshape(flat)
    feed_sums = sum_tensor(jnp.stack([jnp.sum(feed_part * xhat, axis=0), jnp.sum(feed_part, axis=0)]))
    early = as_columns([
        feed_sums[0], feed_sums[1], jnp.sum(dy, axis=0), up_bias_grad.reshape(-1, HEAD_SIZE)])
    early = sum_cores(jnp.concatenate([up_grad, down_grad, early], axis=1))
    after = early
    early = sum_fsdp(early)
    pieces = []
    for i in range(seqs):
        o, dq, dkv = attention(queries[i:i + 1], attended_grad[i:i + 1], gathered[i], after)
        after = early
        pieces.append((
            o, dq, lax.psum_scatter(dkv, "context", scatter_dimension=0, tiled=True)[0]))
    attended = jnp.concatenate([p[0] for p in pieces])
    query_grad = jnp.concatenate([p[1] for p in pieces])
    own = jnp.concatenate([p[2] for p in pieces], axis=1)
    attended = attended.reshape(tokens, width)
    terms = mm(attended, output_weight, 1, 0) + feed_terms
    branches = sum_pair(terms.astype(bf16))
    layer_output = (x + branches + bias_o + bias_d).astype(bf16)
    output_grad = mm(dy_bf, attended, 0, 0)

    query_back = rotate(query_grad, even, -ahead, -behind)
    key_back = rotate(own[0].astype(f32), even, -ahead, -behind)
    projected_grad = jnp.concatenate(
        [query_back.astype(bf16), key_back.astype(bf16), own[1]],
        axis=-1,
    ).reshape(tokens, 3 * width)
    heads_grad = mm(normed_a, projected_grad, 0, 0)
    heads_bias_grad = jnp.sum(projected_grad.astype(f32), axis=0)
    heads_part = mm(projected_grad, heads_weight, 1, 1)

    combined = sum_pair((heads_part * gain_a + feed_part * gain_f).astype(bf16))
    input_grad = dy + scale * (
        combined
        - jnp.mean(combined, axis=-1, keepdims=True)
        - xhat * jnp.mean(combined * xhat, axis=-1, keepdims=True)
    )

    early = sum_context(early, (0, 1))
    up_out = early[:, :hidden_width].astype(f32)
    down_out = early[:, hidden_width:2 * hidden_width].astype(f32).T
    gain_f_out, shift_f_out, bias_out, up_bias_out = vectors_of(
        early[:, 2 * hidden_width:], [share] * 3 + [hidden_width // parts])

    head_sums = sum_tensor(
        jnp.stack([jnp.sum(heads_part * xhat, axis=0), jnp.sum(heads_part, axis=0)]))
    late = as_columns([
        head_sums[0], head_sums[1], heads_bias_grad.reshape(3, heads, HEAD_SIZE)])
    late = jnp.concatenate([heads_grad, output_grad, late], axis=1)
    late = sum_context(sum_fsdp(sum_cores(late)), (1, 0))
    heads_out = late[:, :3 * width].astype(f32).reshape(share, 3, width)
    output_out = late[:, 3 * width:4 * width].astype(f32).T
    gain_a_out, shift_a_out, heads_bias_out = vectors_of(
        late[:, 4 * width:], [share] * 2 + [3 * width // parts])
    return (
        layer_output.reshape(seqs, rows, model),
        input_grad.reshape(seqs, rows, model),
        gain_a_out,
        shift_a_out,
        heads_out,
        heads_bias_out.reshape(query_key_value_bias.shape),
        output_out,
        bias_out,
        gain_f_out,
        shift_f_out,
        up_out,
        up_bias_out.reshape(up_projection_bias.shape),
        down_out,
        bias_out,
    )


def solution(mesh):
    in_specs = (
        P("fsdp", "context", None),
        P("fsdp"),
        P("fsdp"),
        P("fsdp", None, "tensor"),
        P(None, "tensor", "fsdp"),
        P("tensor", "fsdp"),
        P("fsdp"),
        P("fsdp"),
        P("fsdp"),
        P("fsdp", "tensor"),
        P("tensor", "fsdp"),
        P("tensor", "fsdp"),
        P("fsdp"),
        P("fsdp", "context", None),
    )
    out_specs = (
        P("fsdp", "context", None),
        P("fsdp", "context", None),
        P("fsdp"),
        P("fsdp"),
        P("fsdp", None, "tensor"),
        P(None, "tensor", "fsdp"),
        P("tensor", "fsdp"),
        P("fsdp"),
        P("fsdp"),
        P("fsdp"),
        P("fsdp", "tensor"),
        P("tensor", "fsdp"),
        P("tensor", "fsdp"),
        P("fsdp"),
    )
    return jax.shard_map(
        per_device, mesh=mesh, in_specs=in_specs, out_specs=out_specs, check_vma=False
    )
```

```python
import math

import jax
import jax.numpy as jnp
from jax import lax
from jax.experimental import pallas as pl
from jax.experimental.pallas import tpu as pltpu
from jax.sharding import PartitionSpec as P

HEAD_SIZE = 64
ROT = 16
PAIR = 2 * HEAD_SIZE


norm_eps = 1e-05
rotary_base = 10000.0
masked_score = -1e30


def dot(a, b, ca, cb):
    return lax.dot_general(a, b, (((ca,), (cb,)), ((), ())), preferred_element_type=jnp.float32)


def attention_kernel(
    members, half, q_ref, do_ref, kv_ref, after_ref, o_ref, dq_ref, dkv_ref,
    qs, dos, scores, probs, offsets, top, total, acc, dkv
):
    both = 2 * half
    blocks = members // 2
    member = lax.axis_index("context")
    lane = lax.broadcasted_iota(jnp.int32, (half, PAIR), 1)
    first = lane < HEAD_SIZE
    zero = jnp.zeros((half, PAIR), jnp.bfloat16)
    for side in range(2):
        q = q_ref[0, side * half:(side + 1) * half, :]
        g = do_ref[0, side * half:(side + 1) * half, :]
        qs[side, 0:half, :] = jnp.where(first, q, zero)
        qs[side, half:both, :] = jnp.where(first, zero, q)
        dos[side, 0:half, :] = jnp.where(first, g, zero)
        dos[side, half:both, :] = jnp.where(first, zero, g)
    row = lax.broadcasted_iota(jnp.int32, (both, both), 0)
    column = lax.broadcasted_iota(jnp.int32, (both, both), 1)
    offsets[...] = row - jnp.where(column >= half, column - half, column)
    top[...] = jnp.full(top.shape, masked_score, jnp.float32)
    total[...] = jnp.zeros(total.shape, jnp.float32)
    acc[...] = jnp.zeros(acc.shape, jnp.float32)
    dkv[...] = jnp.zeros(dkv.shape, jnp.float32)

    low_jobs = (member + 2) // 2
    jobs = 2 * blocks + 1

    def partial_job(t):
        low = t < low_jobs
        block = jnp.where(low, t, t - low_jobs)
        side = jnp.where(low, 0, 1)
        query_base = jnp.where(low, member, 2 * members - 1 - member) * half
        key_base = jnp.where(low, 0, members * half) + block * both
        first_member = jnp.where(low, 2 * block, members - 1 - 2 * block)
        second_member = jnp.where(low, 2 * block + 1, members - 2 - 2 * block)
        return side, side, first_member, second_member, query_base - key_base

    def load(which, part, a, b):
        return jnp.concatenate([kv_ref[a, which, 0, part], kv_ref[b, which, 0, part]], axis=0)

    def score_job(t, side, part, a, b, limit):
        s = dot(load(0, part, a, b), qs[side], 1, 1)
        if limit is not None:
            s = jnp.where(offsets[...] <= limit, s, masked_score)
        scores[t] = s
        top[side] = jnp.maximum(top[side], jnp.max(s, axis=0, keepdims=True))

    def prob_job(t, side, part, a, b):
        p = jnp.exp(scores[t] - top[side])
        total[side] += jnp.sum(p, axis=0, keepdims=True)
        p = p.astype(jnp.bfloat16)
        probs[t] = p
        acc[side] += dot(load(1, part, a, b), p, 0, 0)

    def back_job(t, side, part, a, b):
        p = probs[t]
        k = load(0, part, a, b)
        dp = dot(load(1, part, a, b), dos[side], 1, 1)
        ds = (p.astype(jnp.float32) * (dp - total[side])).astype(jnp.bfloat16)
        acc[side] += dot(k, ds, 0, 0)
        dk = dot(ds, qs[side], 1, 0)
        dv = dot(p, dos[side], 1, 0)
        dkv[a, 0, part] += dk[:half]
        dkv[b, 0, part] += dk[half:]
        dkv[a, 1, part] += dv[:half]
        dkv[b, 1, part] += dv[half:]

    def run(job, masked):
        @pl.loop(0, blocks)
        def _(t):
            job(t, 1, 0, 2 * t, 2 * t + 1, *((None,) if masked else ()))

        @pl.loop(0, blocks + 1)
        def _(t):
            side, part, a, b, limit = partial_job(t)
            job(t + blocks, side, part, a, b, *((limit,) if masked else ()))

    run(score_job, True)
    run(prob_job, False)
    for side in range(2):
        inverse = 1.0 / total[side]
        o = acc[side] * inverse
        g = jnp.transpose(dos[side].astype(jnp.float32))
        total[side] = jnp.sum(o * g, axis=0, keepdims=True) * inverse
        dos[side] = jnp.transpose(g * inverse).astype(jnp.bfloat16)
        o = jnp.transpose(o)
        o_ref[0, side * half:(side + 1) * half, :] = jnp.where(
            first, o[:half], o[half:]).astype(o_ref.dtype)
    acc[...] = jnp.zeros(acc.shape, jnp.float32)
    run(back_job, False)
    for side in range(2):
        dq = jnp.transpose(acc[side] * (1.0 / math.sqrt(HEAD_SIZE)))
        dq_ref[0, side * half:(side + 1) * half, :] = jnp.where(
            first, dq[:half], dq[half:]).astype(dq_ref.dtype)
    dkv_ref[:, :, 0] = dkv[...].astype(dkv_ref.dtype)


def attention(queries, grads, keys_values, after):
    seqs, rows, width = queries.shape
    members = keys_values.shape[0]
    half = rows // 2
    both = 2 * half
    keys_values = keys_values.reshape(members, 2, seqs, 2, half, width)
    row_spec = pl.BlockSpec((1, rows, PAIR), lambda s, p: (s, 0, p))
    kv_spec = pl.BlockSpec((members, 2, 1, 2, half, PAIR), lambda s, p: (0, 0, s, 0, 0, p))
    jobs = members + 1
    work = seqs * (width // PAIR) * jobs * both * both * PAIR * 2
    out = pl.pallas_call(
        lambda *refs: attention_kernel(members, half, *refs),
        grid=(seqs, width // PAIR),
        in_specs=[row_spec, row_spec, kv_spec, pl.BlockSpec(memory_space=pl.ANY)],
        out_specs=[row_spec, row_spec, kv_spec],
        out_shape=[
            jax.ShapeDtypeStruct(queries.shape, jnp.bfloat16),
            jax.ShapeDtypeStruct(queries.shape, jnp.float32),
            jax.ShapeDtypeStruct(keys_values.shape, jnp.bfloat16),
        ],
        scratch_shapes=[
            pltpu.VMEM((2, both, PAIR), jnp.bfloat16),
            pltpu.VMEM((2, both, PAIR), jnp.bfloat16),
            pltpu.VMEM((jobs, both, both), jnp.float32),
            pltpu.VMEM((jobs, both, both), jnp.bfloat16),
            pltpu.VMEM((both, both), jnp.int32),
            pltpu.VMEM((2, 1, both), jnp.float32),
            pltpu.VMEM((2, 1, both), jnp.float32),
            pltpu.VMEM((2, PAIR, both), jnp.float32),
            pltpu.VMEM((members, 2, 2, half, PAIR), jnp.float32),
        ],
        compiler_params=pltpu.CompilerParams(vmem_limit_bytes=50 * 1024 * 1024),
        cost_estimate=pl.CostEstimate(
            flops=work * 6,
            bytes_accessed=2 * 2 * keys_values.size + 8 * queries.size,
            transcendentals=seqs * (width // PAIR) * jobs * both * both,
        ),
    )(queries, grads, keys_values, after)
    return out[0], out[1], out[2].reshape(members, 2, seqs, rows, width)


def rotate(values, even, ahead, behind):
    half_dim = ROT // 2
    return (
        values * even
        + jnp.roll(values, -half_dim, axis=-1) * ahead
        + jnp.roll(values, half_dim, axis=-1) * behind
    )


def swap(value, axis):
    return lax.ppermute(value, axis, [(0, 1), (1, 0)])


def sibling(value):
    count = lax.axis_size("context")
    return lax.ppermute(value, "context", [(i, i ^ 1) for i in range(count)])


def whole_weight(shard, axis):
    if lax.axis_size("fsdp") != 2:
        return lax.all_gather(shard, "fsdp", axis=axis, tiled=True)
    core = lax.axis_index("context") % 2
    rows = shard.shape[0] // 2
    mine = swap(lax.dynamic_slice_in_dim(shard, core * rows, rows, 0), "fsdp")
    theirs = sibling(mine)
    first = jnp.where(core == 0, mine, theirs)
    second = jnp.where(core == 0, theirs, mine)
    far = jnp.concatenate([first, second], axis=0)
    left = lax.axis_index("fsdp") == 0
    return jnp.concatenate([jnp.where(left, shard, far), jnp.where(left, far, shard)], axis=axis)


def sum_pair(value):
    if lax.axis_size("tensor") != 2:
        return lax.psum(value, "tensor").astype(jnp.float32)
    return value.astype(jnp.float32) + swap(value, "tensor").astype(jnp.float32)


def sum_cores(grad):
    grad = grad.astype(jnp.bfloat16)
    if lax.axis_size("fsdp") != 2:
        return grad
    core = lax.axis_index("context") % 2
    model, columns = grad.shape
    grad = grad.reshape(2, 2, model // 4, columns)
    away = lax.dynamic_slice_in_dim(grad, 1 - core, 1, 1)
    kept = lax.dynamic_slice_in_dim(grad, core, 1, 1)
    total = kept.astype(jnp.float32) + sibling(away).astype(jnp.float32)
    return total.astype(jnp.bfloat16)[:, 0]


def sum_fsdp(grad):
    if lax.axis_size("fsdp") != 2:
        return lax.psum_scatter(grad, "fsdp", scatter_dimension=0, tiled=True)
    side = lax.axis_index("fsdp")
    away = lax.dynamic_slice_in_dim(grad, 1 - side, 1, 0)
    kept = lax.dynamic_slice_in_dim(grad, side, 1, 0)
    total = kept.astype(jnp.float32) + swap(away, "fsdp").astype(jnp.float32)
    return total.astype(jnp.bfloat16)[0]


def sum_context(grad, order):
    if lax.axis_size("fsdp") != 2:
        return lax.psum(grad, "context")
    members = lax.axis_size("context")
    core = lax.axis_index("context") % 2
    groups = [list(range(c, members, 2)) for c in order]
    grad = lax.psum(grad, "context", axis_index_groups=groups)
    theirs = sibling(grad)
    return jnp.concatenate(
        [jnp.where(core == 0, grad, theirs), jnp.where(core == 0, theirs, grad)], axis=0)


def arranged_position(member, within, block_rows, members):
    half_rows = block_rows // 2
    return jnp.where(
        within < half_rows,
        member * half_rows + within,
        (2 * members - 1 - member) * half_rows + within - half_rows,
    )


def mm(a, b, ca, cb):
    return lax.dot_general(a, b, (((ca,), (cb,)), ((), ())), preferred_element_type=jnp.float32)


def per_device(
    layer_input,
    attention_gain,
    attention_shift,
    query_key_value_weight,
    query_key_value_bias,
    attention_output_weight,
    output_bias,
    feed_gain,
    feed_shift,
    up_projection_weight,
    up_projection_bias,
    down_projection_weight,
    down_bias,
    cotangent,
):
    f32, bf16 = jnp.float32, jnp.bfloat16
    seqs, rows, model = layer_input.shape
    tokens = seqs * rows
    parts = lax.axis_size("fsdp")
    members = lax.axis_size("context")
    member = lax.axis_index("context")
    share = model // parts
    width = query_key_value_weight.shape[2]
    heads = width // HEAD_SIZE
    hidden_width = up_projection_weight.shape[1]

    small = [
        attention_gain, attention_shift, query_key_value_bias, output_bias,
        feed_gain, feed_shift, up_projection_bias, down_bias,
    ]
    packed = jnp.concatenate([v.reshape(-1) for v in small])
    if parts == 2:
        far, left = swap(packed, "fsdp"), lax.axis_index("fsdp") == 0
        packed = jnp.stack([jnp.where(left, packed, far), jnp.where(left, far, packed)])
    else:
        packed = lax.all_gather(packed, "fsdp", axis=0)
    whole = []
    start = 0
    for v in small:
        piece = packed[:, start:start + v.size].astype(f32).reshape((parts,) + v.shape)
        start += v.size
        whole.append(jnp.moveaxis(piece, 0, -2).reshape(v.shape[:-1] + (parts * v.shape[-1],)))
    gain_a, shift_a, heads_bias, bias_o, gain_f, shift_f, up_bias, bias_d = whole
    heads_weight = whole_weight(query_key_value_weight.reshape(share, 3 * width), 0)
    heads_weight, up_shard, output_shard, down_shard = lax.optimization_barrier(
        (heads_weight, up_projection_weight, attention_output_weight, down_projection_weight))
    up_weight = whole_weight(up_shard, 0)
    output_weight = whole_weight(output_shard, 1)
    down_weight = whole_weight(down_shard, 1)

    place = arranged_position(member, jnp.arange(rows, dtype=jnp.int32), rows, members)
    frequency = jnp.power(
        jnp.float32(rotary_base), -2.0 * jnp.arange(ROT // 2, dtype=f32) / ROT
    )
    phases = place.astype(f32)[:, None] * frequency[None, :]
    cosine, sine = jnp.cos(phases), jnp.sin(phases)
    rest = HEAD_SIZE - ROT
    none = jnp.zeros((rows, ROT // 2), f32)
    blank = jnp.zeros((rows, rest), f32)
    even = jnp.concatenate([cosine, cosine, jnp.ones((rows, rest), f32)], axis=1)
    even = jnp.tile(even, (1, heads))[None]
    ahead = jnp.tile(jnp.concatenate([-sine, none, blank], axis=1), (1, heads))[None]
    behind = jnp.tile(jnp.concatenate([none, sine, blank], axis=1), (1, heads))[None]

    x = layer_input.astype(f32).reshape(tokens, model)
    dy_bf = cotangent.reshape(tokens, model)
    dy = dy_bf.astype(f32)
    center = x - jnp.mean(x, axis=-1, keepdims=True)
    scale = lax.rsqrt(jnp.mean(center * center, axis=-1, keepdims=True) + norm_eps)
    xhat = center * scale
    normed_a = (xhat * gain_a + shift_a).astype(bf16)
    normed_f = (xhat * gain_f + shift_f).astype(bf16)

    projected = mm(normed_a, heads_weight, 1, 0) + heads_bias.reshape(-1)
    flat = (seqs, rows, width)
    queries, keys, values = (
        projected[:, i * width:(i + 1) * width].reshape(flat) for i in range(3))
    queries = rotate(queries, even, ahead, behind).astype(bf16)
    keys = rotate(keys, even, ahead, behind).astype(bf16)
    values = values.astype(bf16)
    keys, values, normed_f, dy_feed = lax.optimization_barrier((keys, values, normed_f, dy_bf))
    gathered = [
        lax.all_gather(jnp.stack([keys[i:i + 1], values[i:i + 1]]), "context", axis=0)
        for i in range(seqs)]
    queries = queries * jnp.bfloat16(1.0 / math.sqrt(HEAD_SIZE))

    def as_columns(vectors):
        flats = []
        for v in vectors:
            v = v.reshape(v.shape[:-1] + (parts, v.shape[-1] // parts))
            flats.append(jnp.moveaxis(v, -2, 0).reshape(parts, -1))
        flat_all = jnp.concatenate(flats, axis=1)
        columns = -(-flat_all.shape[1] // share)
        flat_all = jnp.pad(flat_all, ((0, 0), (0, columns * share - flat_all.shape[1])))
        return jnp.moveaxis(flat_all.reshape(parts, columns, share), 1, 2).reshape(
            model, columns)

    def vectors_of(columns, sizes):
        flat_all = columns.astype(f32).T.reshape(-1)
        out, start = [], 0
        for size in sizes:
            out.append(flat_all[start:start + size])
            start += size
        return out

    def sum_tensor(v):
        return lax.psum(v, "tensor") if lax.axis_size("tensor") != 2 else v + swap(v, "tensor")

    hidden = mm(normed_f, up_weight, 1, 0) + up_bias.reshape(-1)
    gelu_output, gelu_back = jax.vjp(lambda t: jax.nn.gelu(t, approximate=False), hidden)
    activated = gelu_output.astype(bf16)
    feed_terms = mm(activated, down_weight, 1, 0)
    hidden_grad = gelu_back(mm(dy_feed, down_weight, 1, 1))[0].astype(bf16)
    down_grad = mm(dy_bf, activated, 0, 0)
    up_grad = mm(normed_f, hidden_grad, 0, 0)
    up_bias_grad = jnp.sum(hidden_grad.astype(f32), axis=0)
    feed_part = mm(hidden_grad, up_weight, 1, 1)

    attended_grad = mm(dy_feed, output_weight, 1, 1).astype(bf16).reshape(flat)
    feed_sums = sum_tensor(jnp.stack([jnp.sum(feed_part * xhat, axis=0), jnp.sum(feed_part, axis=0)]))
    early = as_columns([
        feed_sums[0], feed_sums[1], jnp.sum(dy, axis=0), up_bias_grad.reshape(-1, HEAD_SIZE)])
    early = sum_cores(jnp.concatenate([up_grad, down_grad, early], axis=1))
    after = early
    early = sum_fsdp(early)
    pieces = []
    for i in range(seqs):
        o, dq, dkv = attention(queries[i:i + 1], attended_grad[i:i + 1], gathered[i], after)
        pieces.append((
            o, dq, lax.psum_scatter(dkv, "context", scatter_dimension=0, tiled=True)[0]))
    attended = jnp.concatenate([p[0] for p in pieces])
    query_grad = jnp.concatenate([p[1] for p in pieces])
    own = jnp.concatenate([p[2] for p in pieces], axis=1)
    attended = attended.reshape(tokens, width)
    terms = mm(attended, output_weight, 1, 0) + feed_terms
    branches = sum_pair(terms.astype(bf16))
    layer_output = (x + branches + bias_o + bias_d).astype(bf16)
    output_grad = mm(dy_bf, attended, 0, 0)

    query_back = rotate(query_grad, even, -ahead, -behind)
    key_back = rotate(own[0].astype(f32), even, -ahead, -behind)
    projected_grad = jnp.concatenate(
        [query_back.astype(bf16), key_back.astype(bf16), own[1]],
        axis=-1,
    ).reshape(tokens, 3 * width)
    heads_grad = mm(normed_a, projected_grad, 0, 0)
    heads_bias_grad = jnp.sum(projected_grad.astype(f32), axis=0)
    heads_part = mm(projected_grad, heads_weight, 1, 1)

    combined = sum_pair((heads_part * gain_a + feed_part * gain_f).astype(bf16))
    input_grad = dy + scale * (
        combined
        - jnp.mean(combined, axis=-1, keepdims=True)
        - xhat * jnp.mean(combined * xhat, axis=-1, keepdims=True)
    )

    early = sum_context(early, (0, 1))
    up_out = early[:, :hidden_width].astype(f32)
    down_out = early[:, hidden_width:2 * hidden_width].astype(f32).T
    gain_f_out, shift_f_out, bias_out, up_bias_out = vectors_of(
        early[:, 2 * hidden_width:], [share] * 3 + [hidden_width // parts])

    head_sums = sum_tensor(
        jnp.stack([jnp.sum(heads_part * xhat, axis=0), jnp.sum(heads_part, axis=0)]))
    late = as_columns([
        head_sums[0], head_sums[1], heads_bias_grad.reshape(3, heads, HEAD_SIZE)])
    late = jnp.concatenate([heads_grad, output_grad, late], axis=1)
    late = sum_context(sum_fsdp(sum_cores(late)), (1, 0))
    heads_out = late[:, :3 * width].astype(f32).reshape(share, 3, width)
    output_out = late[:, 3 * width:4 * width].astype(f32).T
    gain_a_out, shift_a_out, heads_bias_out = vectors_of(
        late[:, 4 * width:], [share] * 2 + [3 * width // parts])
    return (
        layer_output.reshape(seqs, rows, model),
        input_grad.reshape(seqs, rows, model),
        gain_a_out,
        shift_a_out,
        heads_out,
        heads_bias_out.reshape(query_key_value_bias.shape),
        output_out,
        bias_out,
        gain_f_out,
        shift_f_out,
        up_out,
        up_bias_out.reshape(up_projection_bias.shape),
        down_out,
        bias_out,
    )


def solution(mesh):
    in_specs = (
        P("fsdp", "context", None),
        P("fsdp"),
        P("fsdp"),
        P("fsdp", None, "tensor"),
        P(None, "tensor", "fsdp"),
        P("tensor", "fsdp"),
        P("fsdp"),
        P("fsdp"),
        P("fsdp"),
        P("fsdp", "tensor"),
        P("tensor", "fsdp"),
        P("tensor", "fsdp"),
        P("fsdp"),
        P("fsdp", "context", None),
    )
    out_specs = (
        P("fsdp", "context", None),
        P("fsdp", "context", None),
        P("fsdp"),
        P("fsdp"),
        P("fsdp", None, "tensor"),
        P(None, "tensor", "fsdp"),
        P("tensor", "fsdp"),
        P("fsdp"),
        P("fsdp"),
        P("fsdp"),
        P("fsdp", "tensor"),
        P("tensor", "fsdp"),
        P("tensor", "fsdp"),
        P("fsdp"),
    )
    return jax.shard_map(
        per_device, mesh=mesh, in_specs=in_specs, out_specs=out_specs, check_vma=False
    )
```
